32 devices in a mesh: bead: 8 (over z, y), space: 4 (over x, core).
Axes of the slice: x: 2, y: 2, z: 4, core: 2. Of those that a mesh axis runs over, the one named last changes fastest.
Arguments:
- positions: float32 [8, 3, 65536], P('bead', None, 'space'), may hold values from -5.5 to 5.5
- charges: float32 [65536], P('space'), may hold values from -1 to 1
- polarizability: float32 [65536], P('space'), may hold values from 0.03 to 0.12
- masses: float32 [65536], P('space'), may hold values from 1 to 16
- neighbors: int32 [512, 8], P('space'), may hold values from 0 to 135, as said below
Outputs:
- forces: float32 [8, 3, 65536], P('bead', None, 'space')
- dipoles: float32 [3, 65536], P(None, ('space', 'bead'))
The draws below stay inside these ranges and needn't reach their ends.
Inputs may be any that keep to these rules, and one draw needn't show every extreme that they name: `neighbors`: row t lists 8 different tiles by their index in its domain's extended numbering: the last 4 tiles of the previous domain, the domain's own 128 tiles, the first 4 tiles of the next domain (domains form a cycle). Every listed tile lies within 4 tiles of tile t, and the two tiles at distance exactly 4 on either side are always listed.
All inputs are finite; a program needn't handle non-finite values.
Results may differ from the reference program's by a relative error of at most 0.0001.
Values sent between devices are 32-bit elements; how exact they have to be, the bound alone decides.
A program may use at most 64 MiB of HBM per device.

```python
import math
import jax
import jax.numpy as jnp
from jax import lax

TILE = 128
NBR = 8
HALO_T = 4
ITERS = 3
ATOM_DEV = 16384
BEADS = 8
ATOMS = 65536
TILE_DEV = 128
TILES_ALL = 512


def draw_positions(key, part):
    base_key = jax.random.fold_in(key, 11)
    bead_key = jax.random.fold_in(key, 12)
    base = jnp.clip(jax.random.normal(base_key, (1, 3, ATOMS), jnp.float32), -4.0, 4.0)
    spread = jnp.clip(0.3 * jax.random.normal(bead_key, (BEADS, 3, ATOMS), jnp.float32), -1.5, 1.5)
    return base + spread


def draw_neighbors(key, part):
    inner_count = 2 * HALO_T - 1
    scores = jax.random.randint(jax.random.fold_in(key, 21), (TILES_ALL, inner_count), 0, 1 << 20)
    scores = scores * inner_count + jnp.arange(inner_count, dtype=jnp.int32)[None, :]
    ranking = jnp.argsort(scores, axis=1).astype(jnp.int32)
    chosen = ranking[:, :NBR - 2] - (HALO_T - 1)
    extremes = jnp.broadcast_to(jnp.array([-HALO_T, HALO_T], jnp.int32), (TILES_ALL, 2))
    offsets = jnp.concatenate([extremes[:, :1], chosen, extremes[:, 1:]], axis=1)
    local_tile = (jnp.arange(TILES_ALL, dtype=jnp.int32) % TILE_DEV)[:, None]
    return (local_tile + HALO_T + offsets).astype(jnp.int32)


def block_levels(key, shape, split, low, largest):
    loudness = 1.0
    for axis_at, parts in split:
        steps = jax.random.uniform(jax.random.fold_in(jax.random.fold_in(key, 6), axis_at), (parts,), jnp.float32, low / len(split), largest / len(split))
        loudness = loudness * jnp.repeat(jnp.exp(steps), shape[axis_at] // parts).reshape((-1,) + (1,) * (len(shape) - 1 - axis_at))
    return loudness


def setup_inputs(seed: int = 0) -> dict:
    key_list = jax.random.split(jax.random.key(seed), 6)
    positions = draw_positions(jax.random.fold_in(key_list[5], 71), 0)
    charges = jnp.clip(jax.random.uniform(key_list[1], (ATOMS,), jnp.float32, -1.0, 1.0) * block_levels(key_list[1], (ATOMS,), ((0, 4),), -0.4, 0.0), -1.0, 1.0)
    polarizability = jnp.clip(jnp.exp(math.log(0.12) - 1.3862944 * jax.random.uniform(key_list[2], (ATOMS,), jnp.float32) ** block_levels(key_list[2], (ATOMS,), ((0, 4),), -0.2, 0.2)), 0.03, 0.12)
    masses = jnp.clip(jnp.exp(math.log(16.0) - 2.7725887 * jax.random.uniform(key_list[3], (ATOMS,), jnp.float32) ** block_levels(key_list[3], (ATOMS,), ((0, 4),), -0.2, 0.2)), 1.0, 16.0)
    neighbors = draw_neighbors(jax.random.fold_in(key_list[5], 71), 0)
    return dict(positions=positions, charges=charges, polarizability=polarizability, masses=masses, neighbors=neighbors)


REPULSION = 0.2
SPRING = 0.1


def repulsion_kernel(targets, sources):
    displace = targets[:, :, :, None] - sources[:, :, None, :]
    weight = jnp.exp(-0.5 * jnp.sum(displace * displace, axis=0))
    return REPULSION * jnp.sum(weight[None] * displace, axis=3)


def charge_kernel(targets, sources, charge):
    displace = targets[:, :, :, None] - sources[:, :, None, :]
    weight = jnp.exp(-0.25 * jnp.sum(displace * displace, axis=0)) * charge[0][:, None, :]
    return jnp.sum(weight[None] * displace, axis=3)


def dipole_kernel(targets, sources, dipole):
    displace = targets[:, :, :, None] - sources[:, :, None, :]
    weight = jnp.exp(-0.25 * jnp.sum(displace * displace, axis=0))
    spread_dip = dipole[:, :, None, :]
    projected = jnp.sum(displace * spread_dip, axis=0)
    return jnp.sum(weight[None] * (0.25 * displace * projected[None] - 0.5 * spread_dip), axis=3)


def grouped(kernel, targets, sources):
    tile_count = targets.shape[1]
    group_size = math.gcd(tile_count, 4)

    def split_tiles(tensor):
        return jnp.moveaxis(tensor.reshape(tensor.shape[0], tile_count // group_size, group_size, tensor.shape[2]), 1, 0)

    pieces = tuple(split_tiles(tensor) for tensor in (targets,) + tuple(sources))
    result = lax.map(lambda member: kernel(*member), pieces)
    return jnp.moveaxis(result, 0, 1).reshape(3, tile_count, targets.shape[2])


def tile_table(neighbors):
    tile_total = neighbors.shape[0]
    tiles_domain = ATOM_DEV // TILE
    tile_rows = jnp.arange(tile_total, dtype=jnp.int32)
    domain_start = (tile_rows // tiles_domain) * tiles_domain
    return ((domain_start[:, None] + neighbors - HALO_T) % tile_total).astype(jnp.int32)


def gather_tiles(field, tile_map):
    channels = field.shape[0]
    tiles = field.reshape(channels, tile_map.shape[0], TILE)
    picked = jnp.take(tiles, tile_map, axis=1)
    return picked.reshape(channels, tile_map.shape[0], tile_map.shape[1] * TILE)


def reference(positions, charges, polarizability, masses, neighbors):
    tile_map = tile_table(neighbors)
    tile_total = tile_map.shape[0]

    def bead_forces(coords):
        targets = coords.reshape(3, tile_total, TILE)
        sources = gather_tiles(coords, tile_map)
        return grouped(repulsion_kernel, targets, (sources,)).reshape(3, ATOMS)

    short_range = lax.map(bead_forces, positions)
    cycle_sum = jnp.roll(positions, 1, axis=0) + jnp.roll(positions, -1, axis=0) - 2.0 * positions
    spring = SPRING * masses[None, None, :] * cycle_sum
    centroid = jnp.sum(positions, axis=0) / BEADS
    cent_tiles = centroid.reshape(3, tile_total, TILE)
    cent_sources = gather_tiles(centroid, tile_map)
    charge_sources = gather_tiles(charges[None], tile_map)
    permanent = grouped(charge_kernel, cent_tiles, (cent_sources, charge_sources)).reshape(3, ATOMS)

    def induced(dipole_now):
        return grouped(dipole_kernel, cent_tiles, (cent_sources, gather_tiles(dipole_now, tile_map))).reshape(3, ATOMS)

    dipoles = polarizability[None] * permanent
    for sweep_index in range(ITERS):
        dipoles = polarizability[None] * (permanent + induced(dipoles))
    pulled = charges[None] * induced(dipoles)
    forces = short_range + spring + pulled[None]
    return forces, dipoles
```

```python
import functools

import jax
import jax.numpy as jnp
from jax import lax
from jax.experimental import pallas as pl
from jax.experimental.pallas import tpu as pltpu
from jax.sharding import PartitionSpec as P

TILE = 128
NBR = 8
HALO_T = 4
ITERS = 3
REPULSION = 0.2
SPRING = 0.1
LOG2E = 1.4426950408889634
SHORT_K = 0.5 * LOG2E
CENT_K = 0.25 * LOG2E
F32 = jnp.float32
BF16 = jnp.bfloat16
VMEM = pl.BlockSpec(memory_space=pltpu.VMEM)
SMEM = pl.BlockSpec(memory_space=pltpu.SMEM)


def at(tile):
    return pl.ds(pl.multiple_of(tile * TILE, TILE), TILE)


def rows(block):
    return lax.broadcasted_iota(jnp.int32, block.shape, 0)


def pieces(block, count):
    parts = []
    for _ in range(count):
        top = block.astype(BF16).astype(F32)
        parts.append(top)
        block = block - top
    return parts


def target_features(points, k):
    row, norm = rows(points), jnp.sum(points * points, axis=0, keepdims=True)
    high, mid, low = pieces(jnp.where(row == 3, -k * norm, jnp.where(row == 4, 1.0, points)), 3)
    return jnp.concatenate([high, high, mid, mid, high, low], axis=0).astype(BF16)


def source_features(points, k):
    row, norm = rows(points), jnp.sum(points * points, axis=0, keepdims=True)
    high, mid, low = pieces(
        jnp.where(row == 3, 1.0, jnp.where(row == 4, -k * norm, 2 * k * points)), 3
    )
    return jnp.concatenate([high, mid, high, mid, low, high], axis=0).astype(BF16)


def two_parts(block):
    return jnp.concatenate(pieces(block, 2), axis=0).astype(BF16)


def missing_tile(near, row):
    total = sum(range(2 * HALO_T + 1))
    for n in range(NBR):
        total = total - (near[row, n] - row)
    return total


def listed_tile(ref, t, n, missing):
    if n == 0:
        return ref[:, at(t)]
    if n == NBR - 1:
        return ref[:, at(t + NBR)]
    return lax.select(n < missing, ref[:, at(t + n)], ref[:, at(t + n + 1)])


def side_by_side(ref, t, n, missing):
    return jnp.concatenate(
        [listed_tile(ref, t, n, missing), listed_tile(ref, t, n + 1, missing)], axis=1
    )


def pair_weights(sources, target):
    power = lax.dot_general(
        sources, target, (((0,), (0,)), ((), ())), preferred_element_type=F32
    )
    weight = jnp.exp2(power)
    high = weight.astype(BF16)
    return high, (weight - high.astype(F32)).astype(BF16)


def weighted(values, high, low):
    return jnp.dot(values, high, preferred_element_type=F32) + jnp.dot(
        values, low, preferred_element_type=F32
    )


def joined(total):
    half = total.shape[0] // 2
    return total[:half] + total[half:]


def unrolled(count, step, body):
    while count % step:
        step //= 2

    def group(g, carry):
        for u in range(step):
            body(g * step + u)
        return carry

    lax.fori_loop(0, count // step, group, 0)


def fill_points(wide, points):
    wide[...] = jnp.zeros_like(wide)
    wide[0:3, :] = points


def short_prepare(e, wide, features, values):
    points = wide[:, at(e)]
    features[:, at(e)] = source_features(points, SHORT_K)
    values[:, at(e)] = two_parts(jnp.where(rows(points) == 3, 1.0, points))


def short_tile(t, missing, wide, features, values):
    points = wide[:, at(t + HALO_T)]
    target = target_features(points, SHORT_K)
    total = jnp.zeros((16, TILE), F32)
    for n in range(0, NBR, 2):
        high, low = pair_weights(side_by_side(features, t, n, missing), target)
        total = total + weighted(side_by_side(values, t, n, missing), high, low)
    total = joined(total)
    return REPULSION * (points * total[3:4] - total)


def field_values(e, cent, dip, values):
    points, moment = cent[:, at(e)], dip[:, at(e)]
    row = rows(points)
    along = jnp.sum(points * moment, axis=0, keepdims=True)
    block = jnp.where(row == 3, along, moment)
    block = block + pltpu.roll(block, 4, 0)
    first = block * jnp.where(row < 4, 1.0, points[0:1])
    second = block * jnp.where(row < 4, points[1:2], points[2:3])
    values[:, at(e)] = two_parts(jnp.concatenate([first, second], axis=0))


def field_tile(t, missing, cent, values, g_high, g_low):
    total = jnp.zeros((32, TILE), F32)
    for n in range(0, NBR, 2):
        kept = pl.ds(pl.multiple_of((t * NBR + n) * TILE, 2 * TILE), 2 * TILE)
        total = total + weighted(side_by_side(values, t, n, missing), g_high[kept, :], g_low[kept, :])
    total = joined(total)
    points = cent[:, at(t + HALO_T)]
    row = rows(points)
    signed = jnp.where(row == 3, -1.0, points)
    signed = signed + pltpu.roll(signed, 4, 0)
    first, second = signed * total[0:8], signed * total[8:16]

    def low_rows(block):
        return jnp.sum(jnp.where(row < 4, block, 0.0), axis=0, keepdims=True)

    def high_rows(block):
        return jnp.sum(jnp.where(row < 4, 0.0, block), axis=0, keepdims=True)

    turned = jnp.where(
        row == 0, high_rows(first), jnp.where(row == 1, low_rows(second), high_rows(second))
    )
    field = 0.25 * (points * low_rows(first) - turned) - 0.5 * total[0:8]
    return jnp.where(row < 3, field, 0.0)


def cent_prepare(e, cent, charge, features, values):
    points = cent[:, at(e)]
    features[:, at(e)] = source_features(points, CENT_K)
    values[:, at(e)] = two_parts(jnp.where(rows(points) == 3, 1.0, points) * charge[:, at(e)])


def permanent_tile(t, missing, cent, features, values, g_high, g_low):
    points = cent[:, at(t + HALO_T)]
    target = target_features(points, CENT_K)
    total = jnp.zeros((16, TILE), F32)
    for n in range(0, NBR, 2):
        kept = pl.ds(pl.multiple_of((t * NBR + n) * TILE, 2 * TILE), 2 * TILE)
        high, low = pair_weights(side_by_side(features, t, n, missing), target)
        g_high[kept, :] = high
        g_low[kept, :] = low
        total = total + weighted(side_by_side(values, t, n, missing), high, low)
    total = joined(total)
    return jnp.where(rows(points) < 3, points * total[3:4] - total, 0.0)


def step_kernel(
    beads, spaces, near, pos, charge, alpha, masses, out, dip_out,
    ext, wide, features, values, charge_ext, cent, cent_charge, cent_features, cent_values,
    dip, dip_values, g_high, g_low, permanent, moments, pull_own,
    halo_in, charge_in, spring_in, share_in, rim_in, pull_in,
    halo_send, halo_recv, charge_send, charge_recv, spring_send, spring_recv,
    share_send, share_recv, rim_send, rim_recv, pull_send, pull_recv,
):
    length = pos.shape[1]
    tiles, rim = length // TILE, HALO_T * TILE
    own_tiles = tiles // beads
    own = own_tiles * TILE
    bead, space = lax.axis_index("bead"), lax.axis_index("space")
    base = bead * own_tiles

    def send(source, target, send_sem, recv_sem, where):
        copy = pltpu.make_async_remote_copy(
            src_ref=source, dst_ref=target, send_sem=send_sem, recv_sem=recv_sem,
            device_id=where, device_id_type=pl.DeviceIdType.MESH,
        )
        copy.start()
        return copy

    def bead_at(distance):
        return (lax.rem(bead + distance + beads, beads), space)

    def space_at(distance):
        return (bead, lax.rem(space + distance + spaces, spaces))

    following = (lax.rem(bead + 1, beads), lax.rem(space + (bead + 1) // beads, spaces))
    behind = bead + beads - 1
    preceding = (lax.rem(behind, beads), lax.rem(space + spaces + behind // beads - 1, spaces))

    edges = ((pl.ds(length - rim, rim), 1), (pl.ds(0, rim), -1))
    halos = []
    for side, (edge, way) in enumerate(edges):
        halos.append(send(pos.at[:, edge], halo_in.at[side], halo_send.at[side], halo_recv.at[side], space_at(way)))
        halos.append(send(charge.at[:, edge], charge_in.at[side], charge_send.at[side], charge_recv.at[side], space_at(way)))

    def copy_own(t):
        ext[:, at(t + HALO_T)] = pos[:, at(t)]
        charge_ext[:, at(t + HALO_T)] = charge[:, at(t)]

    unrolled(tiles, 8, copy_own)
    for copy in halos:
        copy.wait()
    for side, start in enumerate((0, length + rim)):
        ext[:, start : start + rim] = halo_in[side]
        charge_ext[:, start : start + rim] = charge_in[side]
    shares = []
    for o in range(1, beads):
        peer = bead_at(o)
        part = pl.ds(pl.multiple_of(peer[0] * own, TILE), own + 2 * rim)
        shares.append(send(ext.at[:, part], share_in.at[o - 1], share_send.at[o - 1], share_recv.at[o - 1], peer))
    springs = [
        send(pos, spring_in.at[side], spring_send.at[side], spring_recv.at[side], bead_at(way))
        for side, way in enumerate((1, -1))
    ]
    fill_points(wide, ext[...])
    unrolled(tiles + 2 * HALO_T, 4, lambda e: short_prepare(e, wide, features, values))

    def short_part(start, count):
        def body(i):
            t = start + i
            out[:, at(t)] = short_tile(t, missing_tile(near, t), wide, features, values)[0:3]

        unrolled(count, 4, body)

    piece = max(tiles // 8, 1)
    rounds = ITERS + 1
    first = tiles - (rounds + 1) * piece
    short_part(0, first)
    for copy in shares:
        copy.wait()
    cent[...] = jnp.zeros_like(cent)
    dip[...] = jnp.zeros_like(dip)

    def center(e):
        total = ext[:, at(base + e)]
        for o in range(1, beads):
            total = total + share_in[o - 1, :, at(e)]
        cent[0:3, at(e)] = total / beads
        cent_charge[:, at(e)] = charge_ext[:, at(base + e)]

    def local_missing(t):
        return missing_tile(near, base + t)

    unrolled(own_tiles + 2 * HALO_T, 4, center)
    unrolled(
        own_tiles + 2 * HALO_T, 4,
        lambda e: cent_prepare(e, cent, cent_charge, cent_features, cent_values),
    )

    def start_tile(t):
        found = permanent_tile(t, local_missing(t), cent, cent_features, cent_values, g_high, g_low)[0:3]
        permanent[:, at(t)] = found
        moments[0, :, at(t)] = alpha[:, at(base + t)] * found

    unrolled(own_tiles, 4, start_tile)

    def sweep(r, carry):
        copies = [
            send(moments.at[r, :, pl.ds(own - rim, rim)], rim_in.at[r, 0], rim_send.at[r, 0], rim_recv.at[r, 0], following),
            send(moments.at[r, :, pl.ds(0, rim)], rim_in.at[r, 1], rim_send.at[r, 1], rim_recv.at[r, 1], preceding),
        ]
        short_part(first + r * piece, piece)

        def own_moment(t):
            dip[0:3, at(t + HALO_T)] = moments[r, :, at(t)]

        unrolled(own_tiles, 4, own_moment)
        for copy in copies:
            copy.wait()
        dip[0:3, 0:rim] = rim_in[r, 0]
        dip[0:3, rim + own : 2 * rim + own] = rim_in[r, 1]
        unrolled(own_tiles + 2 * HALO_T, 4, lambda e: field_values(e, cent, dip, dip_values))

        def field(t):
            found = field_tile(t, local_missing(t), cent, dip_values, g_high, g_low)[0:3]
            moments[r + 1, :, at(t)] = alpha[:, at(base + t)] * (permanent[:, at(t)] + found)
            pull_own[:, at(t)] = charge[:, at(base + t)] * found

        unrolled(own_tiles, 4, field)
        return carry

    lax.fori_loop(0, rounds, sweep, 0)
    pulls = [
        send(pull_own, pull_in.at[o - 1], pull_send.at[o - 1], pull_recv.at[o - 1], bead_at(o))
        for o in range(1, beads)
    ]
    dip_out[...] = moments[ITERS]
    short_part(tiles - piece, piece)
    for copy in springs:
        copy.wait()

    def spring(t):
        own_at = at(t)
        bent = spring_in[0, :, own_at] + spring_in[1, :, own_at] - 2.0 * pos[:, own_at]
        out[:, own_at] = out[:, own_at] + SPRING * masses[:, own_at] * bent

    unrolled(tiles, 8, spring)
    for copy in pulls:
        copy.wait()

    def add_pull(t):
        out[:, at(base + t)] = out[:, at(base + t)] + pull_own[:, at(t)]
        for o in range(1, beads):
            from_tile = lax.rem(bead - o + beads, beads) * own_tiles
            out[:, at(from_tile + t)] = out[:, at(from_tile + t)] + pull_in[o - 1, :, at(t)]

    unrolled(own_tiles, 1, add_pull)


def shaped(*shape):
    return jax.ShapeDtypeStruct(shape, F32)


def per_device(positions, charges, polarizability, masses, neighbors):
    length = positions.shape[2]
    beads, spaces = lax.axis_size("bead"), lax.axis_size("space")
    rim = HALO_T * TILE
    own = length // beads
    full, wide, kept = length + 2 * rim, own + 2 * rim, own * NBR
    peers, rounds = beads - 1, ITERS + 1
    dma = pltpu.SemaphoreType.DMA
    forces, dipoles = pl.pallas_call(
        functools.partial(step_kernel, beads, spaces),
        out_shape=(shaped(3, length), shaped(3, own)),
        in_specs=[SMEM] + [VMEM] * 4,
        out_specs=(VMEM, VMEM),
        scratch_shapes=[
            pltpu.VMEM((3, full), F32),
            pltpu.VMEM((8, full), F32),
            pltpu.VMEM((48, full), BF16),
            pltpu.VMEM((16, full), BF16),
            pltpu.VMEM((1, full), F32),
            pltpu.VMEM((8, wide), F32),
            pltpu.VMEM((1, wide), F32),
            pltpu.VMEM((48, wide), BF16),
            pltpu.VMEM((16, wide), BF16),
            pltpu.VMEM((8, wide), F32),
            pltpu.VMEM((32, wide), BF16),
            pltpu.VMEM((kept, TILE), BF16),
            pltpu.VMEM((kept, TILE), BF16),
            pltpu.VMEM((3, own), F32),
            pltpu.VMEM((rounds + 1, 3, own), F32),
            pltpu.VMEM((3, own), F32),
            pltpu.VMEM((2, 3, rim), F32),
            pltpu.VMEM((2, 1, rim), F32),
            pltpu.VMEM((2, 3, length), F32),
            pltpu.VMEM((peers, 3, wide), F32),
            pltpu.VMEM((rounds, 2, 3, rim), F32),
            pltpu.VMEM((peers, 3, own), F32),
            dma((2,)), dma((2,)), dma((2,)), dma((2,)), dma((2,)), dma((2,)),
            dma((peers,)), dma((peers,)), dma((rounds, 2)), dma((rounds, 2)), dma((peers,)), dma((peers,)),
        ],
        compiler_params=pltpu.CompilerParams(vmem_limit_bytes=48 << 20, has_side_effects=True),
    )(neighbors, positions[0], charges[None], polarizability[None], masses[None])
    return forces[None], dipoles


def solution(mesh):
    in_specs = (P("bead", None, "space"), P("space"), P("space"), P("space"), P("space", None))
    out_specs = (P("bead", None, "space"), P(None, ("space", "bead")))
    return jax.shard_map(
        per_device, mesh=mesh, in_specs=in_specs, out_specs=out_specs, check_vma=False
    )
```

```python
import functools

import jax
import jax.numpy as jnp
from jax import lax
from jax.experimental import pallas as pl
from jax.experimental.pallas import tpu as pltpu
from jax.sharding import PartitionSpec as P

TILE = 128
NBR = 8
HALO_T = 4
ITERS = 3
REPULSION = 0.2
SPRING = 0.1
LOG2E = 1.4426950408889634
SHORT_K = 0.5 * LOG2E
CENT_K = 0.25 * LOG2E
F32 = jnp.float32
BF16 = jnp.bfloat16
VMEM = pl.BlockSpec(memory_space=pltpu.VMEM)
SMEM = pl.BlockSpec(memory_space=pltpu.SMEM)


def at(tile):
    return pl.ds(pl.multiple_of(tile * TILE, TILE), TILE)


def rows(block):
    return lax.broadcasted_iota(jnp.int32, block.shape, 0)


def pieces(block, count):
    parts = []
    for _ in range(count):
        top = block.astype(BF16).astype(F32)
        parts.append(top)
        block = block - top
    return parts


def target_features(points, k):
    row, norm = rows(points), jnp.sum(points * points, axis=0, keepdims=True)
    high, mid, low = pieces(jnp.where(row == 3, -k * norm, jnp.where(row == 4, 1.0, points)), 3)
    return jnp.concatenate([high, high, mid, mid, high, low], axis=0).astype(BF16)


def source_features(points, k):
    row, norm = rows(points), jnp.sum(points * points, axis=0, keepdims=True)
    high, mid, low = pieces(
        jnp.where(row == 3, 1.0, jnp.where(row == 4, -k * norm, 2 * k * points)), 3
    )
    return jnp.concatenate([high, mid, high, mid, low, high], axis=0).astype(BF16)


def two_parts(block):
    return jnp.concatenate(pieces(block, 2), axis=0).astype(BF16)


def missing_tile(near, row):
    total = sum(range(2 * HALO_T + 1))
    for n in range(NBR):
        total = total - (near[row, n] - row)
    return total


def listed_tile(ref, t, n, missing):
    if n == 0:
        return ref[:, at(t)]
    if n == NBR - 1:
        return ref[:, at(t + NBR)]
    return lax.select(n < missing, ref[:, at(t + n)], ref[:, at(t + n + 1)])


def side_by_side(ref, t, n, missing):
    return jnp.concatenate(
        [listed_tile(ref, t, n, missing), listed_tile(ref, t, n + 1, missing)], axis=1
    )


def pair_weights(sources, target):
    power = lax.dot_general(
        sources, target, (((0,), (0,)), ((), ())), preferred_element_type=F32
    )
    weight = jnp.exp2(power)
    high = weight.astype(BF16)
    return high, (weight - high.astype(F32)).astype(BF16)


def weighted(values, high, low):
    return jnp.dot(values, high, preferred_element_type=F32) + jnp.dot(
        values, low, preferred_element_type=F32
    )


def joined(total):
    half = total.shape[0] // 2
    return total[:half] + total[half:]


def unrolled(count, step, body):
    while count % step:
        step //= 2

    def group(g, carry):
        for u in range(step):
            body(g * step + u)
        return carry

    lax.fori_loop(0, count // step, group, 0)


def fill_points(wide, points):
    wide[...] = jnp.zeros_like(wide)
    wide[0:3, :] = points


def short_prepare(e, wide, features, values):
    points = wide[:, at(e)]
    features[:, at(e)] = source_features(points, SHORT_K)
    values[:, at(e)] = two_parts(jnp.where(rows(points) == 3, 1.0, points))


def short_tile(t, missing, wide, features, values):
    points = wide[:, at(t + HALO_T)]
    target = target_features(points, SHORT_K)
    total = jnp.zeros((16, TILE), F32)
    for n in range(0, NBR, 2):
        high, low = pair_weights(side_by_side(features, t, n, missing), target)
        total = total + weighted(side_by_side(values, t, n, missing), high, low)
    total = joined(total)
    return REPULSION * (points * total[3:4] - total)


def field_values(e, cent, dip, values):
    points, moment = cent[:, at(e)], dip[:, at(e)]
    row = rows(points)
    along = jnp.sum(points * moment, axis=0, keepdims=True)
    block = jnp.where(row == 3, along, moment)
    block = block + pltpu.roll(block, 4, 0)
    first = block * jnp.where(row < 4, 1.0, points[0:1])
    second = block * jnp.where(row < 4, points[1:2], points[2:3])
    values[:, at(e)] = two_parts(jnp.concatenate([first, second], axis=0))


def field_tile(t, missing, cent, values, g_high, g_low):
    total = jnp.zeros((32, TILE), F32)
    for n in range(0, NBR, 2):
        kept = pl.ds(pl.multiple_of((t * NBR + n) * TILE, 2 * TILE), 2 * TILE)
        total = total + weighted(side_by_side(values, t, n, missing), g_high[kept, :], g_low[kept, :])
    total = joined(total)
    points = cent[:, at(t + HALO_T)]
    row = rows(points)
    signed = jnp.where(row == 3, -1.0, points)
    signed = signed + pltpu.roll(signed, 4, 0)
    first, second = signed * total[0:8], signed * total[8:16]

    def low_rows(block):
        return jnp.sum(jnp.where(row < 4, block, 0.0), axis=0, keepdims=True)

    def high_rows(block):
        return jnp.sum(jnp.where(row < 4, 0.0, block), axis=0, keepdims=True)

    turned = jnp.where(
        row == 0, high_rows(first), jnp.where(row == 1, low_rows(second), high_rows(second))
    )
    field = 0.25 * (points * low_rows(first) - turned) - 0.5 * total[0:8]
    return jnp.where(row < 3, field, 0.0)


def cent_prepare(e, cent, charge, features, values):
    points = cent[:, at(e)]
    features[:, at(e)] = source_features(points, CENT_K)
    values[:, at(e)] = two_parts(jnp.where(rows(points) == 3, 1.0, points) * charge[:, at(e)])


def permanent_tile(t, missing, cent, features, values, g_high, g_low):
    points = cent[:, at(t + HALO_T)]
    target = target_features(points, CENT_K)
    total = jnp.zeros((16, TILE), F32)
    for n in range(0, NBR, 2):
        kept = pl.ds(pl.multiple_of((t * NBR + n) * TILE, 2 * TILE), 2 * TILE)
        high, low = pair_weights(side_by_side(features, t, n, missing), target)
        g_high[kept, :] = high
        g_low[kept, :] = low
        total = total + weighted(side_by_side(values, t, n, missing), high, low)
    total = joined(total)
    return jnp.where(rows(points) < 3, points * total[3:4] - total, 0.0)


def step_kernel(
    beads, spaces, near, pos, charge, alpha, masses, out, dip_out,
    ext, wide, features, values, charge_ext, cent, cent_charge, cent_features, cent_values,
    dip, dip_values, g_high, g_low, permanent, moments, pull_own,
    halo_in, charge_in, spring_in, share_in, rim_in, pull_in,
    halo_send, halo_recv, charge_send, charge_recv, spring_send, spring_recv,
    share_send, share_recv, rim_send, rim_recv, pull_send, pull_recv,
):
    length = pos.shape[1]
    tiles, rim = length // TILE, HALO_T * TILE
    own_tiles = tiles // beads
    own = own_tiles * TILE
    bead, space = lax.axis_index("bead"), lax.axis_index("space")
    base = bead * own_tiles

    def send(source, target, send_sem, recv_sem, where):
        copy = pltpu.make_async_remote_copy(
            src_ref=source, dst_ref=target, send_sem=send_sem, recv_sem=recv_sem,
            device_id=where, device_id_type=pl.DeviceIdType.MESH,
        )
        copy.start()
        return copy

    def bead_at(distance):
        return (lax.rem(bead + distance + beads, beads), space)

    def space_at(distance):
        return (bead, lax.rem(space + distance + spaces, spaces))

    following = (lax.rem(bead + 1, beads), lax.rem(space + (bead + 1) // beads, spaces))
    behind = bead + beads - 1
    preceding = (lax.rem(behind, beads), lax.rem(space + spaces + behind // beads - 1, spaces))

    edges = ((pl.ds(length - rim, rim), 1), (pl.ds(0, rim), -1))
    halos = []
    for side, (edge, way) in enumerate(edges):
        halos.append(send(pos.at[:, edge], halo_in.at[side], halo_send.at[side], halo_recv.at[side], space_at(way)))
        halos.append(send(charge.at[:, edge], charge_in.at[side], charge_send.at[side], charge_recv.at[side], space_at(way)))

    def copy_own(t):
        ext[:, at(t + HALO_T)] = pos[:, at(t)]
        charge_ext[:, at(t + HALO_T)] = charge[:, at(t)]

    unrolled(tiles, 8, copy_own)
    for copy in halos:
        copy.wait()
    for side, start in enumerate((0, length + rim)):
        ext[:, start : start + rim] = halo_in[side]
        charge_ext[:, start : start + rim] = charge_in[side]
    shares = []
    for o in range(1, beads):
        peer = bead_at(o)
        part = pl.ds(pl.multiple_of(peer[0] * own, TILE), own + 2 * rim)
        shares.append(send(ext.at[:, part], share_in.at[o - 1], share_send.at[o - 1], share_recv.at[o - 1], peer))
    springs = [
        send(pos, spring_in.at[side], spring_send.at[side], spring_recv.at[side], bead_at(way))
        for side, way in enumerate((1, -1))
    ]
    fill_points(wide, ext[...])
    unrolled(tiles + 2 * HALO_T, 8, lambda e: short_prepare(e, wide, features, values))

    def short_part(start, count):
        def body(i):
            t = start + i
            out[:, at(t)] = short_tile(t, missing_tile(near, t), wide, features, values)[0:3]

        unrolled(count, 16, body)

    piece = max(tiles // 8, 1)
    rounds = ITERS + 1
    first = tiles - (rounds + 1) * piece
    short_part(0, first)
    for copy in shares:
        copy.wait()
    cent[...] = jnp.zeros_like(cent)
    dip[...] = jnp.zeros_like(dip)

    def center(e):
        total = ext[:, at(base + e)]
        for o in range(1, beads):
            total = total + share_in[o - 1, :, at(e)]
        cent[0:3, at(e)] = total / beads
        cent_charge[:, at(e)] = charge_ext[:, at(base + e)]

    def local_missing(t):
        return missing_tile(near, base + t)

    unrolled(own_tiles + 2 * HALO_T, 8, center)
    unrolled(
        own_tiles + 2 * HALO_T, 8,
        lambda e: cent_prepare(e, cent, cent_charge, cent_features, cent_values),
    )

    def start_tile(t):
        found = permanent_tile(t, local_missing(t), cent, cent_features, cent_values, g_high, g_low)[0:3]
        permanent[:, at(t)] = found
        moments[0, :, at(t)] = alpha[:, at(base + t)] * found

    unrolled(own_tiles, 16, start_tile)

    def sweep(r, carry):
        copies = [
            send(moments.at[r, :, pl.ds(own - rim, rim)], rim_in.at[r, 0], rim_send.at[r, 0], rim_recv.at[r, 0], following),
            send(moments.at[r, :, pl.ds(0, rim)], rim_in.at[r, 1], rim_send.at[r, 1], rim_recv.at[r, 1], preceding),
        ]
        short_part(first + r * piece, piece)

        def own_moment(t):
            dip[0:3, at(t + HALO_T)] = moments[r, :, at(t)]

        unrolled(own_tiles, 4, own_moment)
        for copy in copies:
            copy.wait()
        dip[0:3, 0:rim] = rim_in[r, 0]
        dip[0:3, rim + own : 2 * rim + own] = rim_in[r, 1]
        unrolled(own_tiles + 2 * HALO_T, 8, lambda e: field_values(e, cent, dip, dip_values))

        def field(t):
            found = field_tile(t, local_missing(t), cent, dip_values, g_high, g_low)[0:3]
            moments[r + 1, :, at(t)] = alpha[:, at(base + t)] * (permanent[:, at(t)] + found)
            pull_own[:, at(t)] = charge[:, at(base + t)] * found

        unrolled(own_tiles, 16, field)
        return carry

    lax.fori_loop(0, rounds, sweep, 0)
    pulls = [
        send(pull_own, pull_in.at[o - 1], pull_send.at[o - 1], pull_recv.at[o - 1], bead_at(o))
        for o in range(1, beads)
    ]
    dip_out[...] = moments[ITERS]
    short_part(tiles - piece, piece)
    for copy in springs:
        copy.wait()

    def spring(t):
        own_at = at(t)
        bent = spring_in[0, :, own_at] + spring_in[1, :, own_at] - 2.0 * pos[:, own_at]
        out[:, own_at] = out[:, own_at] + SPRING * masses[:, own_at] * bent

    unrolled(tiles, 8, spring)
    for copy in pulls:
        copy.wait()

    def add_pull(t):
        out[:, at(base + t)] = out[:, at(base + t)] + pull_own[:, at(t)]
        for o in range(1, beads):
            from_tile = lax.rem(bead - o + beads, beads) * own_tiles
            out[:, at(from_tile + t)] = out[:, at(from_tile + t)] + pull_in[o - 1, :, at(t)]

    unrolled(own_tiles, 4, add_pull)


def shaped(*shape):
    return jax.ShapeDtypeStruct(shape, F32)


def per_device(positions, charges, polarizability, masses, neighbors):
    length = positions.shape[2]
    beads, spaces = lax.axis_size("bead"), lax.axis_size("space")
    rim = HALO_T * TILE
    own = length // beads
    full, wide, kept = length + 2 * rim, own + 2 * rim, own * NBR
    peers, rounds = beads - 1, ITERS + 1
    dma = pltpu.SemaphoreType.DMA
    forces, dipoles = pl.pallas_call(
        functools.partial(step_kernel, beads, spaces),
        out_shape=(shaped(3, length), shaped(3, own)),
        in_specs=[SMEM] + [VMEM] * 4,
        out_specs=(VMEM, VMEM),
        scratch_shapes=[
            pltpu.VMEM((3, full), F32),
            pltpu.VMEM((8, full), F32),
            pltpu.VMEM((48, full), BF16),
            pltpu.VMEM((16, full), BF16),
            pltpu.VMEM((1, full), F32),
            pltpu.VMEM((8, wide), F32),
            pltpu.VMEM((1, wide), F32),
            pltpu.VMEM((48, wide), BF16),
            pltpu.VMEM((16, wide), BF16),
            pltpu.VMEM((8, wide), F32),
            pltpu.VMEM((32, wide), BF16),
            pltpu.VMEM((kept, TILE), BF16),
            pltpu.VMEM((kept, TILE), BF16),
            pltpu.VMEM((3, own), F32),
            pltpu.VMEM((rounds + 1, 3, own), F32),
            pltpu.VMEM((3, own), F32),
            pltpu.VMEM((2, 3, rim), F32),
            pltpu.VMEM((2, 1, rim), F32),
            pltpu.VMEM((2, 3, length), F32),
            pltpu.VMEM((peers, 3, wide), F32),
            pltpu.VMEM((rounds, 2, 3, rim), F32),
            pltpu.VMEM((peers, 3, own), F32),
            dma((2,)), dma((2,)), dma((2,)), dma((2,)), dma((2,)), dma((2,)),
            dma((peers,)), dma((peers,)), dma((rounds, 2)), dma((rounds, 2)), dma((peers,)), dma((peers,)),
        ],
        compiler_params=pltpu.CompilerParams(vmem_limit_bytes=48 << 20, has_side_effects=True),
    )(neighbors, positions[0], charges[None], polarizability[None], masses[None])
    return forces[None], dipoles


def solution(mesh):
    in_specs = (P("bead", None, "space"), P("space"), P("space"), P("space"), P("space", None))
    out_specs = (P("bead", None, "space"), P(None, ("space", "bead")))
    return jax.shard_map(
        per_device, mesh=mesh, in_specs=in_specs, out_specs=out_specs, check_vma=False
    )
```
